32 devices in a mesh: grp: 2 (over x), chan: 16 (over z, y, core).
Axes of the slice: x: 2, y: 2, z: 4, core: 2. Of those that a mesh axis runs over, the one named last changes fastest.
Arguments:
- voltages: bfloat16 [4096, 64, 512], P('chan', 'grp'), parts along dimension 1, may hold values from -6 to 6
- exponents: int32 [64], P('grp'), parts along dimension 0, may hold values from 0 to 2, as said below
- pairs: int32 [128, 2], replicated, may hold values from 0 to 31, as said below
Outputs:
- visibilities: bfloat16 [64, 128, 2, 128, 128], P(('grp', 'chan')), parts along dimension 0
The draws below stay inside these ranges and needn't reach their ends.
There are 2 independent parts, one for each index of `grp`. The reference program is written for one: setup_inputs(seed, part) draws one part's arguments, and reference() takes and returns one part's arrays. A program takes and returns all parts, laid end to end along the dimension named above; an argument that names none is the same for every part. Nothing has to cross between parts.
Inputs may be any that keep to these rules, and one draw needn't show every extreme that they name: exponents are whole numbers. The 128 pairs are distinct and each has first member at most its second.
All inputs are finite; a program needn't handle non-finite values.
Results may differ from the reference program's by a relative error of at most 0.001.
Values may be sent and summed in bfloat16 or wider, within the bound.
A program may use at most 192 MiB of HBM per device.

```python
import jax
import jax.numpy as jnp
from jax import lax

NA = 4096
PANEL = 128
CHANNELS = 32
NT = 256
NBLK = 128


def draw_exponents(key, part):
    index = jnp.arange(CHANNELS)
    flips = jax.random.randint(key, (CHANNELS,), 0, 2)
    flips = jnp.where(index == 0, 1, jnp.where(index == CHANNELS - 1, 0, flips))
    return (2 * (CHANNELS - 1 - index) // CHANNELS + flips).astype(jnp.int32)


def draw_pairs(key, part):
    panels = NA // PANEL
    count = panels * panels
    index = jnp.arange(count)
    scores = jax.random.randint(key, (count,), 0, 1 << 20) * count + index
    valid = index // panels <= index % panels
    scores = jnp.where(valid, scores, (1 << 30) + index)
    scores = jnp.where(index == panels - 1, -1, scores)
    chosen = jnp.argsort(scores)[:NBLK]
    return jnp.stack([chosen // panels, chosen % panels], axis=1).astype(jnp.int32)


def level_of(stream_key, extent, shards, least, high):
    def one(dim, shards_of):
        steps = jax.random.uniform(jax.random.fold_in(jax.random.fold_in(stream_key, 6), dim), (shards_of,), jnp.float32, least / len(shards), high / len(shards))
        return jnp.repeat(jnp.exp(steps), extent[dim] // shards_of).reshape((-1,) + (1,) * (len(extent) - dim - 1))

    loudness = one(*shards[0])
    for cut in shards[1:]:
        loudness = loudness * one(*cut)
    return loudness


def noise(key, extent, deviation, limit, cuts=(), dtype=jnp.bfloat16):
    array = deviation * jax.random.normal(key, extent, jnp.float32)
    if cuts:
        array = array * level_of(key, extent, cuts, -0.22, 0.18)
    return jnp.clip(array, -limit, limit).astype(dtype)


def setup_inputs(seed: int = 0, part: int = 0) -> dict:
    key_of = jax.random.split(jax.random.key(seed), 4)
    part_splits = jax.random.split(jax.random.fold_in(key_of[3], part), 4)
    voltages = noise(part_splits[0], (NA, CHANNELS, 2 * NT), 1.0, 6.0, ((0, 16),))
    exponents = draw_exponents(jax.random.fold_in(jax.random.fold_in(key_of[3], part), 71), part)
    pairs = draw_pairs(jax.random.fold_in(key_of[3], 71), part)
    return dict(voltages=voltages, exponents=exponents, pairs=pairs)


def reference(voltages, exponents, pairs):
    gain = jnp.exp2(-exponents.astype(jnp.float32)).astype(jnp.bfloat16)
    scaled = voltages * gain[None, :, None]
    wide = scaled.astype(jnp.float32)
    power = lax.optimization_barrier(jnp.sum(wide * wide, axis=(1, 2)))
    mean_power = power / (CHANNELS * NT)
    rows = mean_power.reshape(NA // PANEL, PANEL)
    left_power = rows[pairs[:, 0]]
    right_power = rows[pairs[:, 1]]
    denom = jnp.sqrt(NT * left_power[:, :, None] * right_power[:, None, :])

    def one_channel(plane):
        panels = plane.astype(jnp.float32).reshape(NA // PANEL, PANEL, 2 * NT)
        rotated = jnp.concatenate([panels[:, :, NT:], -panels[:, :, :NT]], axis=2)
        left_real = panels[pairs[:, 0]]
        left_imag = rotated[pairs[:, 0]]
        right = panels[pairs[:, 1]]
        real_part = jnp.einsum('kit,kjt->kij', left_real, right, precision=lax.Precision.HIGHEST)
        imag_part = jnp.einsum('kit,kjt->kij', left_imag, right, precision=lax.Precision.HIGHEST)
        raw = jnp.stack([real_part, imag_part], axis=1)
        return (raw / denom[:, None, :, :]).astype(jnp.bfloat16)
    return lax.map(one_channel, jnp.moveaxis(scaled, 1, 0))
```

```python
import functools
import math

import jax
import jax.numpy as jnp
from jax import lax
from jax.experimental import pallas as pl
from jax.experimental.pallas import tpu as pltpu
from jax.sharding import PartitionSpec as P

PANEL = 128
NT = 256
GROUP = 16
VMEM_LIMIT = 56 * 1024 * 1024


def block_product(left, right, col, row):
    half = left.shape[1] // 2
    turned = jnp.concatenate([-right[:, half:], right[:, :half]], axis=1)
    both = jnp.concatenate([right, turned], axis=0)
    raw = lax.dot_general(left, both, (((1,), (1,)), ((), ())), preferred_element_type=jnp.float32)
    scale = col * row
    return (raw[:, :PANEL] * scale).astype(jnp.bfloat16), (raw[:, PANEL:] * scale).astype(jnp.bfloat16)


def turn_kernel(n, total, x_ref, pow_ref, pairs_ref, late_ref, vis_ref, col_ref, row_ref,
                early, stage, allpow, cols, rows, send, recv, psend, precv, local):
    me = lax.axis_index("chan")
    ants = early.shape[1]
    per = ants // PANEL

    barrier = pltpu.get_barrier_semaphore()

    @pl.loop(1, n)
    def _(off):
        pl.semaphore_signal(barrier, inc=1, device_id={"chan": lax.rem(me + off, n)},
                            device_id_type=pl.DeviceIdType.MESH)

    own_pow = pltpu.make_async_copy(pow_ref, allpow.at[me], local.at[0])
    own_early = pltpu.make_async_copy(x_ref.at[2 * me], early.at[me], local.at[1])
    own_late = pltpu.make_async_copy(x_ref.at[2 * me + 1], late_ref.at[me], local.at[2])
    own_pow.start()
    own_early.start()
    own_late.start()
    pl.semaphore_wait(barrier, n - 1)

    def pow_copy(off):
        return pltpu.make_async_remote_copy(
            src_ref=pow_ref, dst_ref=allpow.at[me], send_sem=psend.at[off], recv_sem=precv.at[off],
            device_id={"chan": lax.rem(me + off, n)}, device_id_type=pl.DeviceIdType.MESH)

    def data_copy(slot, off):
        dst = lax.rem(me + off, n)
        return pltpu.make_async_remote_copy(
            src_ref=x_ref.at[2 * dst + slot], dst_ref=(early, late_ref)[slot].at[me],
            send_sem=send.at[slot, off], recv_sem=recv.at[slot, off],
            device_id={"chan": dst}, device_id_type=pl.DeviceIdType.MESH)

    @pl.loop(1, n)
    def _(off):
        pow_copy(off).start()

    @pl.loop(1, n)
    def _(off):
        data_copy(0, off).start()

    @pl.loop(1, n)
    def _(off):
        data_copy(1, off).start()

    own_pow.wait()

    @pl.loop(1, n)
    def _(off):
        pow_copy(off).wait()

    for d in range(n):
        for h in range(per):
            p = d * per + h
            mean = allpow[d, 0:1, h * PANEL:(h + 1) * PANEL] / total
            rows[p] = jnp.broadcast_to(lax.rsqrt(mean), (8, PANEL))
            cols[p] = jnp.broadcast_to(lax.rsqrt(NT * mean), (PANEL, PANEL)).T
    col_out = pltpu.make_async_copy(cols, col_ref, local.at[3])
    row_out = pltpu.make_async_copy(rows, row_ref, local.at[4])
    col_out.start()
    row_out.start()

    own_early.wait()

    @pl.loop(1, n)
    def _(off):
        data_copy(0, off).wait()

    @pl.loop(0, pairs_ref.shape[0])
    def _(k):
        p, q = pairs_ref[k, 0], pairs_ref[k, 1]
        left = early[p // per, pl.ds(lax.rem(p, per) * PANEL, PANEL), :]
        right = early[q // per, pl.ds(lax.rem(q, per) * PANEL, PANEL), :]
        re, im = block_product(left, right, cols[p], rows[q, 0:1, :])
        stage[k, 0] = re
        stage[k, 1] = im

    vis_out = pltpu.make_async_copy(stage, vis_ref, local.at[5])
    vis_out.start()
    own_late.wait()

    @pl.loop(1, n)
    def _(off):
        data_copy(1, off).wait()

    vis_out.wait()
    col_out.wait()
    row_out.wait()


def finish_kernel(data_ref, vis_ref, cols, rows, pairs_ref, out_ref, stage, sems):
    nblk = pairs_ref.shape[0]
    groups = nblk // GROUP

    def old(g):
        part = pl.ds(g * GROUP, GROUP)
        return pltpu.make_async_copy(vis_ref.at[part], out_ref.at[0, part], sems.at[0, g])

    def new(g):
        part = pl.ds(g * GROUP, GROUP)
        return pltpu.make_async_copy(stage.at[part], out_ref.at[1, part], sems.at[1, g])

    for g in range(groups):
        old(g).start()

    for g in range(groups):
        @pl.loop(g * GROUP, (g + 1) * GROUP, unroll=4)
        def _(k):
            p, q = pairs_ref[k, 0], pairs_ref[k, 1]
            re, im = block_product(data_ref[p], data_ref[q], cols[p], rows[q, 0:1, :])
            stage[k, 0] = re
            stage[k, 1] = im
        new(g).start()

    for g in range(groups):
        old(g).wait()
        new(g).wait()


def on_device(n, voltages, exponents, pairs):
    ants, chans, width = voltages.shape
    assert chans == 2 * n and ants % PANEL == 0
    nblk = pairs.shape[0]
    panels = n * ants // PANEL
    gain = jnp.exp2(-exponents.astype(jnp.float32)).astype(jnp.bfloat16)
    scaled = voltages * gain[None, :, None]
    wide = scaled.astype(jnp.float32)
    power = jnp.sum(wide * wide, axis=(1, 2))
    power = jnp.broadcast_to(power[None, :], (8, ants))
    turned = jnp.swapaxes(scaled, 0, 1)

    hbm = pl.BlockSpec(memory_space=pl.ANY)
    vmem = pl.BlockSpec(memory_space=pltpu.VMEM)
    smem = pl.BlockSpec(memory_space=pltpu.SMEM)
    late, vis, cols, rows = pl.pallas_call(
        functools.partial(turn_kernel, n, float(chans * NT)),
        out_shape=[
            jax.ShapeDtypeStruct((n, ants, width), jnp.bfloat16),
            jax.ShapeDtypeStruct((nblk, 2, PANEL, PANEL), jnp.bfloat16),
            jax.ShapeDtypeStruct((panels, PANEL, PANEL), jnp.float32),
            jax.ShapeDtypeStruct((panels, 8, PANEL), jnp.float32),
        ],
        in_specs=[hbm, vmem, smem],
        out_specs=[hbm, hbm, hbm, hbm],
        scratch_shapes=[
            pltpu.VMEM((n, ants, width), jnp.bfloat16),
            pltpu.VMEM((nblk, 2, PANEL, PANEL), jnp.bfloat16),
            pltpu.VMEM((n, 8, ants), jnp.float32),
            pltpu.VMEM((panels, PANEL, PANEL), jnp.float32),
            pltpu.VMEM((panels, 8, PANEL), jnp.float32),
            pltpu.SemaphoreType.DMA((2, n)),
            pltpu.SemaphoreType.DMA((2, n)),
            pltpu.SemaphoreType.DMA((n,)),
            pltpu.SemaphoreType.DMA((n,)),
            pltpu.SemaphoreType.DMA((6,)),
        ],
        compiler_params=pltpu.CompilerParams(
            collective_id=0, has_side_effects=True, vmem_limit_bytes=VMEM_LIMIT),
        name="turn",
    )(turned, power, pairs)

    return pl.pallas_call(
        finish_kernel,
        out_shape=jax.ShapeDtypeStruct((2, nblk, 2, PANEL, PANEL), jnp.bfloat16),
        in_specs=[vmem, hbm, vmem, vmem, smem],
        out_specs=hbm,
        scratch_shapes=[
            pltpu.VMEM((nblk, 2, PANEL, PANEL), jnp.bfloat16),
            pltpu.SemaphoreType.DMA((2, nblk // GROUP)),
        ],
        compiler_params=pltpu.CompilerParams(vmem_limit_bytes=VMEM_LIMIT),
        name="finish",
    )(late.reshape(panels, PANEL, width), vis, cols, rows, pairs)


def solution(mesh):
    return jax.shard_map(
        functools.partial(on_device, mesh.shape["chan"]),
        mesh=mesh,
        in_specs=(P("chan", "grp", None), P("grp"), P()),
        out_specs=P(("grp", "chan"), None, None, None, None),
        check_vma=False,
    )
```

```python
import functools
import math

import jax
import jax.numpy as jnp
from jax import lax
from jax.experimental import pallas as pl
from jax.experimental.pallas import tpu as pltpu
from jax.sharding import PartitionSpec as P

PANEL = 128
NT = 256
GROUP = 16
VMEM_LIMIT = 56 * 1024 * 1024


def block_product(left, right, col, row):
    half = left.shape[1] // 2
    turned = jnp.concatenate([-right[:, half:], right[:, :half]], axis=1)
    both = jnp.concatenate([right, turned], axis=0)
    raw = lax.dot_general(left, both, (((1,), (1,)), ((), ())), preferred_element_type=jnp.float32)
    scale = col * row
    return (raw[:, :PANEL] * scale).astype(jnp.bfloat16), (raw[:, PANEL:] * scale).astype(jnp.bfloat16)


def turn_kernel(n, total, x_ref, exps_ref, pairs_ref, late_ref, vis_ref, col_ref, row_ref,
                raw, wide, outbox, early, stage, sums, ownpow, allpow, cols, rows,
                send, recv, lsend, lrecv, psend, precv, insem, local):
    me = lax.axis_index("chan")
    pieces, size, chans, width = raw.shape
    ants = pieces * size
    per = ants // PANEL
    lanes = width // 128

    def in_copy(b):
        return pltpu.make_async_copy(x_ref.at[pl.ds(b * size, size)], raw.at[b], insem.at[b])

    for b in range(pieces):
        in_copy(b).start()

    barrier = pltpu.get_barrier_semaphore()

    @pl.loop(1, n)
    def _(off):
        pl.semaphore_signal(barrier, inc=1, device_id={"chan": lax.rem(me + off, n)},
                            device_id_type=pl.DeviceIdType.MESH)

    def pow_copy(off):
        return pltpu.make_async_remote_copy(
            src_ref=ownpow, dst_ref=allpow.at[me], send_sem=psend.at[off], recv_sem=precv.at[off],
            device_id={"chan": lax.rem(me + off, n)}, device_id_type=pl.DeviceIdType.MESH)

    def early_copy(b, off):
        dst = lax.rem(me + off, n)
        part = pl.ds(b * size, size)
        return pltpu.make_async_remote_copy(
            src_ref=outbox.at[2 * dst, part], dst_ref=early.at[me, part],
            send_sem=send.at[b, off], recv_sem=recv.at[b, off],
            device_id={"chan": dst}, device_id_type=pl.DeviceIdType.MESH)

    def late_copy(off):
        dst = lax.rem(me + off, n)
        return pltpu.make_async_remote_copy(
            src_ref=outbox.at[2 * dst + 1], dst_ref=late_ref.at[me],
            send_sem=lsend.at[off], recv_sem=lrecv.at[off],
            device_id={"chan": dst}, device_id_type=pl.DeviceIdType.MESH)

    for b in range(pieces):
        in_copy(b).wait()

        @pl.loop(0, size // 2)
        def _(a):
            for i in range(2):
                row = raw[b, a * 2 + i].astype(jnp.float32)
                at = pl.ds(pl.multiple_of((a * 2 + i) * chans, chans), chans)
                for t in range(lanes):
                    wide[t, at, :] = row[:, t * 128:(t + 1) * 128]

        def channel(c, acc):
            gain = lax.shift_left(jnp.int32(1), 30 - exps_ref[c]).astype(jnp.float32) * 2.0 ** -30
            for t in range(lanes):
                v = wide[t, pl.ds(c, size, stride=chans), :] * gain
                acc = acc + v * v
                outbox[c, b * size:(b + 1) * size, t * 128:(t + 1) * 128] = v.astype(jnp.bfloat16)
            return acc

        acc = lax.fori_loop(0, chans, channel, jnp.zeros((size, 128), jnp.float32))
        sums[b * size:(b + 1) * size, :] = acc
        if b == 0:
            pl.semaphore_wait(barrier, n - 1)

        @pl.loop(1, n)
        def _(off):
            early_copy(b, off).start()

    for h in range(per):
        row = jnp.sum(sums[h * PANEL:(h + 1) * PANEL, :].T, axis=0, keepdims=True)
        ownpow[:, h * PANEL:(h + 1) * PANEL] = jnp.broadcast_to(row, (8, PANEL))

    @pl.loop(1, n)
    def _(off):
        pow_copy(off).start()

    @pl.loop(1, n)
    def _(off):
        late_copy(off).start()

    own_pow = pltpu.make_async_copy(ownpow, allpow.at[me], local.at[0])
    own_early = pltpu.make_async_copy(outbox.at[2 * me], early.at[me], local.at[1])
    own_late = pltpu.make_async_copy(outbox.at[2 * me + 1], late_ref.at[me], local.at[2])
    own_pow.start()
    own_early.start()
    own_late.start()
    own_pow.wait()

    @pl.loop(1, n)
    def _(off):
        pow_copy(off).wait()

    @pl.loop(0, n)
    def _(d):
        for h in range(per):
            p = d * per + h
            mean = allpow[d, 0:1, h * PANEL:(h + 1) * PANEL] / total
            rows[p] = jnp.broadcast_to(lax.rsqrt(mean), (8, PANEL))
            cols[p] = jnp.broadcast_to(lax.rsqrt(NT * mean), (PANEL, PANEL)).T

    col_out = pltpu.make_async_copy(cols, col_ref, local.at[3])
    row_out = pltpu.make_async_copy(rows, row_ref, local.at[4])
    col_out.start()
    row_out.start()
    own_early.wait()

    for b in range(pieces):
        @pl.loop(1, n)
        def _(off):
            early_copy(b, off).wait()

    @pl.loop(0, pairs_ref.shape[1])
    def _(k):
        p, q = pairs_ref[0, k], pairs_ref[1, k]
        left = early[p // per, pl.ds(lax.rem(p, per) * PANEL, PANEL), :]
        right = early[q // per, pl.ds(lax.rem(q, per) * PANEL, PANEL), :]
        re, im = block_product(left, right, cols[p], rows[q, 0:1, :])
        stage[k, 0] = re
        stage[k, 1] = im

    vis_out = pltpu.make_async_copy(stage, vis_ref, local.at[5])
    vis_out.start()
    own_late.wait()

    @pl.loop(1, n)
    def _(off):
        late_copy(off).wait()

    vis_out.wait()
    col_out.wait()
    row_out.wait()


def finish_kernel(data_ref, vis_ref, col_ref, rows, pairs_ref, out_ref, data, cols, first, stage, insem, sems):
    nblk = pairs_ref.shape[1]
    groups = nblk // GROUP

    data_in = pltpu.make_async_copy(data_ref, data, insem.at[groups])
    cols_in = pltpu.make_async_copy(col_ref, cols, insem.at[groups + 1])
    data_in.start()
    cols_in.start()

    def fetch(g):
        part = pl.ds(g * GROUP, GROUP)
        return pltpu.make_async_copy(vis_ref.at[part], first.at[part], insem.at[g])

    def old(g):
        part = pl.ds(g * GROUP, GROUP)
        return pltpu.make_async_copy(first.at[part], out_ref.at[0, part], sems.at[0, g])

    def new(g):
        part = pl.ds(g * GROUP, GROUP)
        return pltpu.make_async_copy(stage.at[part], out_ref.at[1, part], sems.at[1, g])

    for g in range(groups):
        fetch(g).start()
    data_in.wait()
    cols_in.wait()

    for g in range(groups):
        @pl.loop(g * GROUP, (g + 1) * GROUP, unroll=4)
        def _(k):
            p, q = pairs_ref[0, k], pairs_ref[1, k]
            re, im = block_product(data[p], data[q], cols[p], rows[q, 0:1, :])
            stage[k, 0] = re
            stage[k, 1] = im
        new(g).start()
        fetch(g).wait()
        old(g).start()

    for g in range(groups):
        old(g).wait()
        new(g).wait()


def on_device(n, voltages, exponents, pairs):
    ants, chans, width = voltages.shape
    assert chans == 2 * n and ants % PANEL == 0
    nblk = pairs.shape[0]
    panels = n * ants // PANEL
    size = 64
    pieces = ants // size
    pairs = pairs.T

    hbm = pl.BlockSpec(memory_space=pl.ANY)
    vmem = pl.BlockSpec(memory_space=pltpu.VMEM)
    smem = pl.BlockSpec(memory_space=pltpu.SMEM)
    dma = pltpu.SemaphoreType.DMA
    late, vis, cols, rows = pl.pallas_call(
        functools.partial(turn_kernel, n, float(chans * NT)),
        out_shape=[
            jax.ShapeDtypeStruct((n, ants, width), jnp.bfloat16),
            jax.ShapeDtypeStruct((nblk, 2, PANEL, PANEL), jnp.bfloat16),
            jax.ShapeDtypeStruct((panels, PANEL, PANEL), jnp.float32),
            jax.ShapeDtypeStruct((panels, 8, PANEL), jnp.float32),
        ],
        in_specs=[hbm, smem, smem],
        out_specs=[hbm, hbm, hbm, hbm],
        scratch_shapes=[
            pltpu.VMEM((pieces, size, chans, width), jnp.bfloat16),
            pltpu.VMEM((width // 128, size * chans, 128), jnp.float32),
            pltpu.VMEM((chans, ants, width), jnp.bfloat16),
            pltpu.VMEM((n, ants, width), jnp.bfloat16),
            pltpu.VMEM((nblk, 2, PANEL, PANEL), jnp.bfloat16),
            pltpu.VMEM((ants, 128), jnp.float32),
            pltpu.VMEM((8, ants), jnp.float32),
            pltpu.VMEM((n, 8, ants), jnp.float32),
            pltpu.VMEM((panels, PANEL, PANEL), jnp.float32),
            pltpu.VMEM((panels, 8, PANEL), jnp.float32),
            dma((pieces, n)), dma((pieces, n)), dma((n,)), dma((n,)), dma((n,)), dma((n,)),
            dma((pieces,)), dma((6,)),
        ],
        compiler_params=pltpu.CompilerParams(
            collective_id=0, has_side_effects=True, vmem_limit_bytes=VMEM_LIMIT),
        name="turn",
    )(voltages, exponents, pairs)

    return pl.pallas_call(
        finish_kernel,
        out_shape=jax.ShapeDtypeStruct((2, nblk, 2, PANEL, PANEL), jnp.bfloat16),
        in_specs=[hbm, hbm, hbm, vmem, smem],
        out_specs=hbm,
        scratch_shapes=[
            pltpu.VMEM((panels, PANEL, width), jnp.bfloat16),
            pltpu.VMEM((panels, PANEL, PANEL), jnp.float32),
            pltpu.VMEM((nblk, 2, PANEL, PANEL), jnp.bfloat16),
            pltpu.VMEM((nblk, 2, PANEL, PANEL), jnp.bfloat16),
            dma((nblk // GROUP + 2,)),
            dma((2, nblk // GROUP)),
        ],
        compiler_params=pltpu.CompilerParams(vmem_limit_bytes=VMEM_LIMIT),
        name="finish",
    )(late.reshape(panels, PANEL, width), vis, cols, rows, pairs)


def solution(mesh):
    return jax.shard_map(
        functools.partial(on_device, mesh.shape["chan"]),
        mesh=mesh,
        in_specs=(P("chan", "grp", None), P("grp"), P()),
        out_specs=P(("grp", "chan"), None, None, None, None),
        check_vma=False,
    )
```

```python
import functools
import math

import jax
import jax.numpy as jnp
from jax import lax
from jax.experimental import pallas as pl
from jax.experimental.pallas import tpu as pltpu
from jax.sharding import PartitionSpec as P

PANEL = 128
NT = 256
GROUP = 16
VMEM_LIMIT = 56 * 1024 * 1024


def block_product(left, right, col, row):
    half = left.shape[1] // 2
    turned = jnp.concatenate([-right[:, half:], right[:, :half]], axis=1)
    both = jnp.concatenate([right, turned], axis=0)
    raw = lax.dot_general(left, both, (((1,), (1,)), ((), ())), preferred_element_type=jnp.float32)
    scale = col * row
    return (raw[:, :PANEL] * scale).astype(jnp.bfloat16), (raw[:, PANEL:] * scale).astype(jnp.bfloat16)


def turn_kernel(n, total, x_ref, exps_ref, pairs_ref, late_ref, vis_ref, row_ref,
                raw, wide, outbox, early, stage, sums, ownpow, allpow, cols, rows,
                send, recv, lsend, lrecv, psend, precv, insem, local):
    me = lax.axis_index("chan")
    pieces, size, chans, width = raw.shape
    ants = pieces * size
    per = ants // PANEL
    lanes = width // 128

    def in_copy(b):
        return pltpu.make_async_copy(x_ref.at[pl.ds(b * size, size)], raw.at[b], insem.at[b])

    for b in range(pieces):
        in_copy(b).start()

    barrier = pltpu.get_barrier_semaphore()

    @pl.loop(1, n)
    def _(off):
        pl.semaphore_signal(barrier, inc=1, device_id={"chan": lax.rem(me + off, n)},
                            device_id_type=pl.DeviceIdType.MESH)

    def pow_copy(off):
        return pltpu.make_async_remote_copy(
            src_ref=ownpow, dst_ref=allpow.at[me], send_sem=psend.at[off], recv_sem=precv.at[off],
            device_id={"chan": lax.rem(me + off, n)}, device_id_type=pl.DeviceIdType.MESH)

    def early_copy(b, off):
        dst = lax.rem(me + off, n)
        part = pl.ds(b * size, size)
        return pltpu.make_async_remote_copy(
            src_ref=outbox.at[2 * dst, part], dst_ref=early.at[me, part],
            send_sem=send.at[b, off], recv_sem=recv.at[b, off],
            device_id={"chan": dst}, device_id_type=pl.DeviceIdType.MESH)

    def late_copy(off):
        dst = lax.rem(me + off, n)
        return pltpu.make_async_remote_copy(
            src_ref=outbox.at[2 * dst + 1], dst_ref=late_ref.at[me],
            send_sem=lsend.at[off], recv_sem=lrecv.at[off],
            device_id={"chan": dst}, device_id_type=pl.DeviceIdType.MESH)

    for b in range(pieces):
        in_copy(b).wait()

        @pl.loop(0, size // 2)
        def _(a):
            for i in range(2):
                row = raw[b, a * 2 + i].astype(jnp.float32)
                at = pl.ds(pl.multiple_of((a * 2 + i) * chans, chans), chans)
                for t in range(lanes):
                    wide[t, at, :] = row[:, t * 128:(t + 1) * 128]

        def channel(c, acc):
            gain = lax.shift_left(jnp.int32(1), 30 - exps_ref[c]).astype(jnp.float32) * 2.0 ** -30
            for t in range(lanes):
                v = wide[t, pl.ds(c, size, stride=chans), :] * gain
                acc = acc + v * v
                outbox[c, b * size:(b + 1) * size, t * 128:(t + 1) * 128] = v.astype(jnp.bfloat16)
            return acc

        acc = lax.fori_loop(0, chans, channel, jnp.zeros((size, 128), jnp.float32))
        sums[b * size:(b + 1) * size, :] = acc
        if b == 0:
            pl.semaphore_wait(barrier, n - 1)

        @pl.loop(1, n)
        def _(off):
            early_copy(b, off).start()

    for h in range(per):
        row = jnp.sum(sums[h * PANEL:(h + 1) * PANEL, :].T, axis=0, keepdims=True)
        ownpow[:, h * PANEL:(h + 1) * PANEL] = jnp.broadcast_to(row, (8, PANEL))

    @pl.loop(1, n)
    def _(off):
        pow_copy(off).start()

    @pl.loop(1, n)
    def _(off):
        late_copy(off).start()

    own_pow = pltpu.make_async_copy(ownpow, allpow.at[me], local.at[0])
    own_early = pltpu.make_async_copy(outbox.at[2 * me], early.at[me], local.at[1])
    own_late = pltpu.make_async_copy(outbox.at[2 * me + 1], late_ref.at[me], local.at[2])
    own_pow.start()
    own_early.start()
    own_late.start()
    own_pow.wait()

    @pl.loop(1, n)
    def _(off):
        pow_copy(off).wait()

    @pl.loop(0, n)
    def _(d):
        for h in range(per):
            p = d * per + h
            mean = allpow[d, 0:1, h * PANEL:(h + 1) * PANEL] / total
            rows[p] = jnp.broadcast_to(lax.rsqrt(mean), (8, PANEL))
            cols[p] = jnp.broadcast_to(lax.rsqrt(NT * mean), (PANEL, PANEL)).T

    row_out = pltpu.make_async_copy(rows, row_ref, local.at[3])
    row_out.start()
    own_early.wait()

    for b in range(pieces):
        @pl.loop(1, n)
        def _(off):
            early_copy(b, off).wait()

    @pl.loop(0, pairs_ref.shape[1])
    def _(k):
        p, q = pairs_ref[0, k], pairs_ref[1, k]
        left = early[p // per, pl.ds(lax.rem(p, per) * PANEL, PANEL), :]
        right = early[q // per, pl.ds(lax.rem(q, per) * PANEL, PANEL), :]
        re, im = block_product(left, right, cols[p], rows[q, 0:1, :])
        stage[k, 0] = re
        stage[k, 1] = im

    vis_out = pltpu.make_async_copy(stage, vis_ref, local.at[4])
    vis_out.start()
    own_late.wait()

    @pl.loop(1, n)
    def _(off):
        late_copy(off).wait()

    vis_out.wait()
    row_out.wait()


def finish_kernel(data_ref, vis_ref, rows, pairs_ref, out_ref, data, twist, cols, first, stage, insem, sems):
    nblk = pairs_ref.shape[1]
    panels, _, width = data_ref.shape
    half = width // 2
    groups = nblk // GROUP
    loads = insem.shape[0] - groups
    some = panels // loads

    def load(j):
        part = pl.ds(j * some, some)
        return pltpu.make_async_copy(data_ref.at[part], data.at[part], insem.at[groups + j])

    def fetch(g):
        part = pl.ds(g * GROUP, GROUP)
        return pltpu.make_async_copy(vis_ref.at[part], first.at[part], insem.at[g])

    def old(g):
        part = pl.ds(g * GROUP, GROUP)
        return pltpu.make_async_copy(first.at[part], out_ref.at[0, part], sems.at[0, g])

    def new(g):
        part = pl.ds(g * GROUP, GROUP)
        return pltpu.make_async_copy(stage.at[part], out_ref.at[1, part], sems.at[1, g])

    for j in range(loads):
        load(j).start()
    for g in range(groups):
        fetch(g).start()

    table = jnp.concatenate([rows[p, 0:1, :] for p in range(panels)]
                            + [jnp.zeros((PANEL - panels, PANEL), jnp.float32)], axis=0).T * NT ** -0.5
    for p in range(panels):
        cols[p] = jnp.broadcast_to(table[:, p:p + 1], (PANEL, PANEL))

    for j in range(loads):
        load(j).wait()

        @pl.loop(j * some, (j + 1) * some, unroll=2)
        def _(p):
            t = data[p].T
            twist[p, :, :PANEL] = t
            twist[p, :half, PANEL:] = -t[half:]
            twist[p, half:, PANEL:] = t[:half]

    for g in range(groups):
        fetch(g).wait()
        old(g).start()

        @pl.loop(g * GROUP, (g + 1) * GROUP, unroll=GROUP)
        def _(k):
            p, q = pairs_ref[0, k], pairs_ref[1, k]
            raw = jnp.dot(data[p], twist[q], preferred_element_type=jnp.float32)
            scale = cols[p] * rows[q, 0:1, :]
            stage[k, 0] = (raw[:, :PANEL] * scale).astype(jnp.bfloat16)
            stage[k, 1] = (raw[:, PANEL:] * scale).astype(jnp.bfloat16)
        new(g).start()

    for g in range(groups):
        old(g).wait()
        new(g).wait()


def on_device(n, voltages, exponents, pairs):
    ants, chans, width = voltages.shape
    assert chans == 2 * n and ants % PANEL == 0
    nblk = pairs.shape[0]
    panels = n * ants // PANEL
    size = 32
    pieces = ants // size
    pairs = pairs.T

    hbm = pl.BlockSpec(memory_space=pl.ANY)
    vmem = pl.BlockSpec(memory_space=pltpu.VMEM)
    smem = pl.BlockSpec(memory_space=pltpu.SMEM)
    dma = pltpu.SemaphoreType.DMA
    late, vis, rows = pl.pallas_call(
        functools.partial(turn_kernel, n, float(chans * NT)),
        out_shape=[
            jax.ShapeDtypeStruct((n, ants, width), jnp.bfloat16),
            jax.ShapeDtypeStruct((nblk, 2, PANEL, PANEL), jnp.bfloat16),
            jax.ShapeDtypeStruct((panels, 8, PANEL), jnp.float32),
        ],
        in_specs=[hbm, smem, smem],
        out_specs=[hbm, hbm, hbm],
        scratch_shapes=[
            pltpu.VMEM((pieces, size, chans, width), jnp.bfloat16),
            pltpu.VMEM((width // 128, size * chans, 128), jnp.float32),
            pltpu.VMEM((chans, ants, width), jnp.bfloat16),
            pltpu.VMEM((n, ants, width), jnp.bfloat16),
            pltpu.VMEM((nblk, 2, PANEL, PANEL), jnp.bfloat16),
            pltpu.VMEM((ants, 128), jnp.float32),
            pltpu.VMEM((8, ants), jnp.float32),
            pltpu.VMEM((n, 8, ants), jnp.float32),
            pltpu.VMEM((panels, PANEL, PANEL), jnp.float32),
            pltpu.VMEM((panels, 8, PANEL), jnp.float32),
            dma((pieces, n)), dma((pieces, n)), dma((n,)), dma((n,)), dma((n,)), dma((n,)),
            dma((pieces,)), dma((5,)),
        ],
        compiler_params=pltpu.CompilerParams(
            collective_id=0, has_side_effects=True, vmem_limit_bytes=VMEM_LIMIT),
        name="turn",
    )(voltages, exponents, pairs)

    return pl.pallas_call(
        finish_kernel,
        out_shape=jax.ShapeDtypeStruct((2, nblk, 2, PANEL, PANEL), jnp.bfloat16),
        in_specs=[hbm, hbm, vmem, smem],
        out_specs=hbm,
        scratch_shapes=[
            pltpu.VMEM((panels, PANEL, width), jnp.bfloat16),
            pltpu.VMEM((panels, width, 2 * PANEL), jnp.bfloat16),
            pltpu.VMEM((panels, PANEL, PANEL), jnp.float32),
            pltpu.VMEM((nblk, 2, PANEL, PANEL), jnp.bfloat16),
            pltpu.VMEM((nblk, 2, PANEL, PANEL), jnp.bfloat16),
            dma((nblk // GROUP + 4,)),
            dma((2, nblk // GROUP)),
        ],
        compiler_params=pltpu.CompilerParams(vmem_limit_bytes=VMEM_LIMIT),
        name="finish",
    )(late.reshape(panels, PANEL, width), vis, rows, pairs)


def solution(mesh):
    return jax.shard_map(
        functools.partial(on_device, mesh.shape["chan"]),
        mesh=mesh,
        in_specs=(P("chan", "grp", None), P("grp"), P()),
        out_specs=P(("grp", "chan"), None, None, None, None),
        check_vma=False,
    )
```
